512 devices in a mesh: pts: 64 (over x, z_hi, y, core), freq: 8 (over z_lo).
Axes of the slice: x: 4, y: 4, z: 16 (z_hi: 2, z_lo: 8; z = z_hi * 8 + z_lo), core: 2. Of those that a mesh axis runs over, the one named last changes fastest.
Arguments:
- green_src: bfloat16 [24, 2, 128, 16384], P('freq', None, None, 'pts'), may hold values from -1.5 to 1.5
- green_rcv: bfloat16 [24, 2, 128, 16384], P('freq', None, None, 'pts'), may hold values from -1.5 to 1.5
- pairing: int32 [2, 64], replicated, may hold values from 0 to 63, as said below
- freq_index: int32 [24], P('freq'), may hold values from 32 to 63
Outputs:
- hessian: float32 [16384, 2, 256], P(('pts', 'freq'))
The draws below stay inside these ranges and needn't reach their ends.
Inputs may be any that keep to these rules, and one draw needn't show every extreme that they name: Each row pairs the point blocks two by two: pairing[r, pairing[r, b]] = b and pairing[r, b] != b.
All inputs are finite; a program needn't handle non-finite values.
Results may differ from the reference program's by a relative error of at most 0.0003.
Values may be sent and summed in bfloat16 or wider, within the bound.
A program may use at most 64 MiB of HBM per device.

```python
import jax
import jax.numpy as jnp
from jax import lax

SRC = 128
RCV = 128
PTS_DEV = 256
ROUNDS = 2
FBINS = 64
NP = 16384
NF = 24
N_PTS = 64


def draw_pairing(key, part):
    key = jax.random.fold_in(key, 11)

    def single(subkey):
        order = jax.random.permutation(subkey, N_PTS).astype(jnp.int32)
        flipped = order[jnp.arange(N_PTS, dtype=jnp.int32) ^ 1]
        return jnp.zeros((N_PTS,), jnp.int32).at[order].set(flipped)
    return jax.vmap(single)(jax.random.split(key, ROUNDS))


def with_ends(entries, rng, low, top_value):
    index_at = [jax.random.randint(jax.random.fold_in(rng, axis), (), 0, length) for axis, length in enumerate(entries.shape)]
    main_axis = entries.shape.index(max(entries.shape))
    neighbour = index_at[:main_axis] + [(index_at[main_axis] + 1) % entries.shape[main_axis]] + index_at[main_axis + 1:]
    return entries.at[tuple(index_at)].set(low).at[tuple(neighbour)].set(top_value)


def steps_of(key, dims, shards, smallest, high):
    gain = 1.0
    for axis_at, shards_of in shards:
        heights = jax.random.uniform(jax.random.fold_in(jax.random.fold_in(key, 6), axis_at), (shards_of,), jnp.float32, smallest / len(shards), high / len(shards))
        gain = gain * jnp.repeat(jnp.exp(heights), dims[axis_at] // shards_of).reshape((-1,) + (1,) * (len(dims) - 1 - axis_at))
    return gain


def noise(own_key, shape, width, reach, shards=(), kind=jnp.bfloat16):
    values = jax.random.normal(own_key, shape, jnp.float32) * width
    if len(shards) > 0:
        values = steps_of(own_key, shape, shards, -0.22, 0.18) * values
    return jnp.clip(values, min=-reach, max=reach).astype(kind)


def setup_inputs(seed: int = 0) -> dict:
    key_list = jax.random.split(jax.random.key(seed), 5)
    return {
        "green_src": noise(key_list[0], (NF, 2, SRC, NP), 0.25, 1.5, ((0, 8), (3, 64))),
        "green_rcv": noise(key_list[1], (NF, 2, RCV, NP), 0.25, 1.5, ((0, 8), (3, 64))),
        "pairing": draw_pairing(jax.random.fold_in(key_list[4], 71), 0),
        "freq_index": with_ends(jax.random.randint(key_list[3], (NF,), FBINS // 2, FBINS), jax.random.fold_in(key_list[3], 1), FBINS // 2, FBINS - 1).astype(jnp.int32),
    }


def gram_parts(own, other):
    real = jnp.einsum('fsa,fsb->fab', own[:, 0], other[:, 0]) + jnp.einsum('fsa,fsb->fab', own[:, 1], other[:, 1])
    imag = jnp.einsum('fsa,fsb->fab', own[:, 0], other[:, 1]) - jnp.einsum('fsa,fsb->fab', own[:, 1], other[:, 0])
    return real, imag


def reference(green_src, green_rcv, pairing, freq_index):
    weights = ((freq_index.astype(jnp.float32) + 1.0) / FBINS) ** 4
    sources = green_src.astype(jnp.float32)
    receivers = green_rcv.astype(jnp.float32)

    def block_term(pair):
        block, mate = pair
        first = (block * PTS_DEV).astype(jnp.int32)
        second = (mate * PTS_DEV).astype(jnp.int32)
        own_s = lax.dynamic_slice_in_dim(sources, first, PTS_DEV, 3)
        mate_s = lax.dynamic_slice_in_dim(sources, second, PTS_DEV, 3)
        own_r = lax.dynamic_slice_in_dim(receivers, first, PTS_DEV, 3)
        mate_r = lax.dynamic_slice_in_dim(receivers, second, PTS_DEV, 3)
        src_re, src_im = gram_parts(own_s, mate_s)
        rcv_re, rcv_im = gram_parts(own_r, mate_r)
        return jnp.einsum('f,fab->ab', weights, src_re * rcv_re - src_im * rcv_im)

    rounds = []
    blocks = jnp.arange(N_PTS).astype(jnp.int32)
    for step in range(ROUNDS):
        terms = lax.map(block_term, (blocks, pairing[step].astype(jnp.int32)))
        rounds.append(terms.reshape(N_PTS * PTS_DEV, PTS_DEV))
    return jnp.stack(rounds, axis=1)
```

```python
import functools

import jax
import jax.numpy as jnp
from jax import lax
from jax.experimental import pallas as pl
from jax.experimental.pallas import tpu as pltpu
from jax.sharding import PartitionSpec as P

ROUNDS = 2
FBINS = 64
PEERS = 32
SLICE = 16
MESH = pl.DeviceIdType.MESH
CHUNKS = ((1, 0, 256), (0, 0, 128), (0, 128, 128))


def device(x, y_core, z):
    return (x * 16 + lax.div(z, 8) * 8 + y_core, lax.rem(z, 8))


def kernel(
    src_ref, rcv_ref, pair_ref, freq_ref, out_ref,
    w_own, w_got, blocks, slices_a, slices_b, slices_c, picked, mates, terms, right_in, left_in,
    z_send, z_recv, w_send, w_recv, spread_send, spread_recv, back_send, back_recv,
    ring_send, ring_recv,
):
    p, f = lax.axis_index("pts"), lax.axis_index("freq")
    x, zh, yc = lax.div(p, 16), lax.rem(lax.div(p, 8), 2), lax.rem(p, 8)
    z = zh * 8 + f
    me = x * 8 + yc
    slices = (slices_a, slices_b, slices_c)

    def peer(t):
        return (lax.div(t, 8) * 16 + zh * 8 + lax.rem(t, 8), f)

    up, down = device(x, yc, lax.rem(z + 1, 16)), device(x, yc, lax.rem(z + 15, 16))
    barrier = pltpu.get_barrier_semaphore()
    for dz in (4, 12, 1, 15):
        pl.semaphore_signal(
            barrier, inc=1, device_id=device(x, yc, lax.rem(z + dz, 16)), device_id_type=MESH
        )

    @pl.loop(1, PEERS)
    def _(i):
        pl.semaphore_signal(
            barrier, inc=1, device_id=peer(lax.rem(me + i, PEERS)), device_id_type=MESH
        )

    for slot in range(3):
        scaled = (freq_ref[slot].astype(jnp.float32) + 1.0) / FBINS
        scaled = scaled * scaled
        w_own[slot] = jnp.full(w_own.shape[1:], scaled * scaled, jnp.float32)
    pl.semaphore_wait(barrier, PEERS - 1 + 4)

    far = lax.rem(f + 4, 8)

    def meeting(way):
        return (x * 16 + lax.rem(lax.div(f, 4) + way, 2) * 8 + yc, far)

    for number, (place, first, cols) in enumerate(CHUNKS):
        columns = pl.ds(first, cols)
        for slot, way in ((2, lax.rem(f, 2)),) if place else ((0, 0), (1, 1)):
            target = meeting(way)
            if first == 0:
                pltpu.make_async_remote_copy(
                    w_own.at[slot], w_got.at[place, zh], w_send, w_recv.at[place],
                    device_id=target, device_id_type=MESH,
                ).start()
            for side, ref in enumerate((src_ref, rcv_ref)):
                pltpu.make_async_remote_copy(
                    ref.at[slot, :, columns],
                    blocks.at[place, zh, pl.ds(256 * side, 256), columns],
                    z_send.at[side], z_recv.at[number],
                    device_id=target, device_id_type=MESH,
                ).start()

    terms[...] = jnp.zeros_like(terms)
    home = lax.div(far, 4)
    two = lax.rem(zh + home, 2) == lax.rem(f, 2)

    def arrived(ref, sem):
        pltpu.make_async_copy(ref, ref, sem).wait()

    def spread(number):
        place, first, cols = CHUNKS[number]
        columns = pl.ds(first, cols)
        arrived(blocks.at[place, :, :, columns], z_recv.at[number])

        @pl.loop(1, PEERS)
        def _(i):
            t = lax.rem(me + i, PEERS)
            pltpu.make_async_remote_copy(
                blocks.at[place, :, pl.ds(t * SLICE, SLICE), columns],
                slices[number].at[x, :, yc],
                spread_send.at[number], spread_recv.at[number],
                device_id=peer(t), device_id_type=MESH,
            ).start()

        pltpu.make_async_copy(
            blocks.at[place, :, pl.ds(me * SLICE, SLICE), columns],
            slices[number].at[x, :, yc],
            spread_recv.at[number],
        ).start()

    def back(number):
        place, first, cols = CHUNKS[number]
        columns = pl.ds(first, cols)
        arrived(slices[number], spread_recv.at[number])

        def pick(t):
            for r in range(ROUNDS):
                for h in range(2):
                    m = pair_ref[r, lax.div(t, 8) * 16 + h * 8 + lax.rem(t, 8)]
                    picked[place, t, r, h, :, columns] = slices[number][
                        lax.div(m, 16), lax.rem(lax.div(m, 8), 2), lax.rem(m, 8)
                    ]

        @pl.loop(1, PEERS)
        def _(i):
            t = lax.rem(me + i, PEERS)
            pick(t)
            pltpu.make_async_remote_copy(
                picked.at[place, t, :, :, :, columns],
                mates.at[place, :, :, pl.ds(me * SLICE, SLICE), columns],
                back_send.at[number], back_recv.at[number],
                device_id=peer(t), device_id_type=MESH,
            ).start()

        pick(me)
        pltpu.make_async_copy(
            picked.at[place, me, :, :, :, columns],
            mates.at[place, :, :, pl.ds(me * SLICE, SLICE), columns],
            back_recv.at[number],
        ).start()

    def gram(left, right):
        turned = jnp.concatenate([right[128:], -right[:128]], axis=0)
        both = jnp.concatenate([right, turned], axis=1)
        prod = lax.dot_general(
            left, both, (((0,), (0,)), ((), ())), preferred_element_type=jnp.float32
        )
        return prod[:, : right.shape[1]], prod[:, right.shape[1] :]

    def multiply(number):
        place, first, cols = CHUNKS[number]
        columns = pl.ds(first, cols)
        arrived(mates.at[place, :, :, :, columns], back_recv.at[number])
        weight = w_got[place, 0, 0:1, 0:1]

        @pl.loop(0, 2 * ROUNDS)
        def _(i):
            h, r = lax.div(i, ROUNDS), lax.rem(i, ROUNDS)
            src_re, src_im = gram(
                blocks[place, h, pl.ds(0, 256), :], mates[place, r, h, pl.ds(0, 256), columns]
            )
            rcv_re, rcv_im = gram(
                blocks[place, h, pl.ds(256, 256), :], mates[place, r, h, pl.ds(256, 256), columns]
            )
            term = weight * (src_re * rcv_re - src_im * rcv_im)
            terms[pl.ds(h * 8, 8), r, :, columns] += term.reshape(8, 32, cols)

    def finish(number):
        place, first, cols = CHUNKS[number]
        columns = pl.ds(first, cols)
        arrived(blocks.at[place, :, pl.ds(0, 31 * SLICE), columns], spread_send.at[number])
        arrived(picked.at[place, pl.ds(0, 31), :, :, :, columns], back_send.at[number])

    @pl.when(two)
    def _():
        arrived(w_got.at[1], w_recv.at[1])
        spread(0)
        back(0)

    arrived(w_got.at[0], w_recv.at[0])
    spread(1)
    back(1)

    @pl.when(two)
    def _():
        multiply(0)

    spread(2)
    back(2)
    multiply(1)
    multiply(2)

    def up_copy(step, r, source):
        return pltpu.make_async_remote_copy(
            source, right_in.at[step, r], ring_send.at[0, step, r], ring_recv.at[0, step, r],
            device_id=up, device_id_type=MESH,
        )

    def down_copy(step, r, source):
        return pltpu.make_async_remote_copy(
            source, left_in.at[step, r], ring_send.at[1, step, r], ring_recv.at[1, step, r],
            device_id=down, device_id_type=MESH,
        )

    for r in range(ROUNDS):
        up_copy(0, r, terms.at[lax.rem(z + 8, 16), r]).start()
        down_copy(0, r, terms.at[lax.rem(z + 9, 16), r]).start()

    @pl.loop(0, 6)
    def _(s):
        for r in range(ROUNDS):
            up_copy(s, r, right_in.at[s, r]).wait_recv()
            right_in[s, r] += terms[lax.rem(z + 7 - s, 16), r]
            up_copy(s + 1, r, right_in.at[s, r]).start()
            down_copy(s, r, left_in.at[s, r]).wait_recv()
            left_in[s, r] += terms[lax.rem(z + 10 + s, 16), r]
            down_copy(s + 1, r, left_in.at[s, r]).start()

    for r in range(ROUNDS):
        up_copy(6, r, right_in.at[6, r]).wait_recv()
        right_in[6, r] += terms[lax.rem(z + 1, 16), r]
        up_copy(7, r, right_in.at[6, r]).start()
    for r in range(ROUNDS):
        down_copy(6, r, left_in.at[6, r]).wait_recv()
        left_in[6, r] += terms[z, r]
        up_copy(7, r, right_in.at[7, r]).wait_recv()
        out_ref[r] = left_in[6, r] + right_in[7, r]

    @pl.when(two)
    def _():
        finish(0)

    finish(1)
    finish(2)
    arrived(src_ref, z_send.at[0])
    arrived(rcv_ref, z_send.at[1])
    arrived(w_own, w_send)

    @pl.loop(0, 7)
    def _(s):
        for r in range(ROUNDS):
            up_copy(s, r, right_in.at[s, r]).wait_send()
            down_copy(s, r, left_in.at[s, r]).wait_send()

    for r in range(ROUNDS):
        up_copy(7, r, right_in.at[6, r]).wait_send()


def on_device(green_src, green_rcv, pairing, freq_index):
    bf16, f32 = jnp.bfloat16, jnp.float32
    n = len(CHUNKS)
    dma = pltpu.SemaphoreType.DMA
    result = pl.pallas_call(
        kernel,
        out_shape=jax.ShapeDtypeStruct((ROUNDS, 32, 256), f32),
        in_specs=[
            pl.BlockSpec(memory_space=pl.ANY),
            pl.BlockSpec(memory_space=pl.ANY),
            pl.BlockSpec(memory_space=pltpu.SMEM),
            pl.BlockSpec(memory_space=pltpu.SMEM),
        ],
        out_specs=pl.BlockSpec(memory_space=pltpu.VMEM),
        scratch_shapes=[
            pltpu.VMEM((3, 8, 128), f32),
            pltpu.VMEM((2, 2, 8, 128), f32),
            pltpu.VMEM((2, 2, 512, 256), bf16),
            *(pltpu.VMEM((4, 2, 8, SLICE, cols), bf16) for _, _, cols in CHUNKS),
            pltpu.VMEM((2, PEERS, ROUNDS, 2, SLICE, 256), bf16),
            pltpu.VMEM((2, ROUNDS, 2, 512, 256), bf16),
            pltpu.VMEM((16, ROUNDS, 32, 256), f32),
            pltpu.VMEM((8, ROUNDS, 32, 256), f32),
            pltpu.VMEM((7, ROUNDS, 32, 256), f32),
            dma((2,)), dma((n,)), dma, dma((2,)),
            dma((n,)), dma((n,)), dma((n,)), dma((n,)),
            dma((2, 8, ROUNDS)), dma((2, 8, ROUNDS)),
        ],
        compiler_params=pltpu.CompilerParams(
            collective_id=0, has_side_effects=True, vmem_limit_bytes=48 << 20
        ),
    )(green_src.reshape(3, 256, 256), green_rcv.reshape(3, 256, 256), pairing, freq_index)
    return result.swapaxes(0, 1)


def solution(mesh):
    in_specs = (P("freq", None, None, "pts"), P("freq", None, None, "pts"), P(), P("freq"))
    out_specs = P(("pts", "freq"), None, None)
    return jax.shard_map(
        on_device, mesh=mesh, in_specs=in_specs, out_specs=out_specs, check_vma=False
    )
```

```python
import functools

import jax
import jax.numpy as jnp
from jax import lax
from jax.experimental import pallas as pl
from jax.experimental.pallas import tpu as pltpu
from jax.sharding import PartitionSpec as P

ROUNDS = 2
FBINS = 64
PEERS = 32
SLICE = 16
MESH = pl.DeviceIdType.MESH
CHUNKS = ((1, 0), (0, 0), (1, 128), (0, 128))
COLS = 128


def device(x, y_core, z):
    return (x * 16 + lax.div(z, 8) * 8 + y_core, lax.rem(z, 8))


def kernel(src_ref, rcv_ref, pair_ref, freq_ref, out_ref, *scratch):
    n = len(CHUNKS)
    blocks, slices, picked, mates = (scratch[i * n : (i + 1) * n] for i in range(4))
    (
        w_own, w_got, terms, up_in, down_in,
        z_send, z_recv, w_send, w_recv, spread_send, spread_recv, back_send, back_recv,
        ring_send, ring_recv,
    ) = scratch[4 * n :]
    p, f = lax.axis_index("pts"), lax.axis_index("freq")
    x, zh, yc = lax.div(p, 16), lax.rem(lax.div(p, 8), 2), lax.rem(p, 8)
    z = zh * 8 + f
    me = x * 8 + yc

    def peer(t):
        return (lax.div(t, 8) * 16 + zh * 8 + lax.rem(t, 8), f)

    up, down = device(x, yc, lax.rem(z + 1, 16)), device(x, yc, lax.rem(z + 15, 16))
    barrier = pltpu.get_barrier_semaphore()
    for dz in (4, 12, 1, 15):
        pl.semaphore_signal(
            barrier, inc=1, device_id=device(x, yc, lax.rem(z + dz, 16)), device_id_type=MESH
        )

    @pl.loop(1, PEERS)
    def _(i):
        pl.semaphore_signal(
            barrier, inc=1, device_id=peer(lax.rem(me + i, PEERS)), device_id_type=MESH
        )

    for slot in range(3):
        scaled = (freq_ref[slot].astype(jnp.float32) + 1.0) / FBINS
        scaled = scaled * scaled
        w_own[slot] = jnp.full(w_own.shape[1:], scaled * scaled, jnp.float32)
    pl.semaphore_wait(barrier, PEERS - 1 + 4)

    far = lax.rem(f + 4, 8)

    def meeting(way):
        return (x * 16 + lax.rem(lax.div(f, 4) + way, 2) * 8 + yc, far)

    def arrived(ref, sem):
        pltpu.make_async_copy(ref, ref, sem).wait()

    def z_step(number, k):
        place, first = CHUNKS[number]
        slot, row = (2, k) if place else (lax.rem(k, 2), lax.div(k, 2))
        target = meeting(lax.rem(f, 2) if place else slot)
        for side, ref in enumerate((src_ref, rcv_ref)):
            pltpu.make_async_remote_copy(
                ref.at[slot, row, :, pl.ds(first, COLS)],
                blocks[number].at[16 * side + row, zh],
                z_send.at[number, side], z_recv.at[number],
                device_id=target, device_id_type=MESH,
            ).start()

    def z_steps(number, start, count):
        @pl.loop(start, start + count)
        def _(k):
            z_step(number, k)

    def z_between(i, plan):
        for number, start, count in plan:
            before = lax.div((i - 1) * count, PEERS - 1)

            @pl.when(lax.div(i * count, PEERS - 1) > before)
            def _(number=number, k=start + before):
                z_step(number, k)

    def launched(number):
        place, first = CHUNKS[number]
        slots = pl.ds(2, 1) if place else pl.ds(0, 2)
        for side, ref in enumerate((src_ref, rcv_ref)):
            arrived(ref.at[slots, :, :, pl.ds(first, COLS)], z_send.at[number, side])

    for slot, place, way in ((2, 1, lax.rem(f, 2)), (0, 0, 0), (1, 0, 1)):
        pltpu.make_async_remote_copy(
            w_own.at[slot], w_got.at[place, zh], w_send, w_recv.at[place],
            device_id=meeting(way), device_id_type=MESH,
        ).start()
    z_steps(0, 0, 16)
    z_steps(1, 0, 8)
    terms[...] = jnp.zeros_like(terms)
    two = lax.rem(zh + lax.div(far, 4), 2) == lax.rem(f, 2)

    def spread(number, plan=()):
        arrived(blocks[number], z_recv.at[number])

        @pl.loop(1, PEERS)
        def _(i):
            z_between(i, plan)
            t = lax.rem(me + i, PEERS)
            pltpu.make_async_remote_copy(
                blocks[number].at[t], slices[number].at[x, yc],
                spread_send.at[number], spread_recv.at[number],
                device_id=peer(t), device_id_type=MESH,
            ).start()

        pltpu.make_async_copy(
            blocks[number].at[me], slices[number].at[x, yc], spread_recv.at[number]
        ).start()

    def back(number, plan=()):
        arrived(slices[number], spread_recv.at[number])

        def pick(t):
            for r in range(ROUNDS):
                for h in range(2):
                    m = pair_ref[r, lax.div(t, 8) * 16 + h * 8 + lax.rem(t, 8)]
                    picked[number][t, r, h] = slices[number][
                        lax.div(m, 16), lax.rem(m, 8), lax.rem(lax.div(m, 8), 2)
                    ]

        @pl.loop(1, PEERS)
        def _(i):
            z_between(i, plan)
            t = lax.rem(me + i, PEERS)
            pick(t)
            pltpu.make_async_remote_copy(
                picked[number].at[t], mates[number].at[me],
                back_send.at[number], back_recv.at[number],
                device_id=peer(t), device_id_type=MESH,
            ).start()

        pick(me)
        pltpu.make_async_copy(
            picked[number].at[me], mates[number].at[me], back_recv.at[number]
        ).start()

    def gram(left, right):
        turned = jnp.concatenate([right[128:], -right[:128]], axis=0)
        both = jnp.concatenate([right, turned], axis=1)
        prod = lax.dot_general(
            left, both, (((0,), (0,)), ((), ())), preferred_element_type=jnp.float32
        )
        return prod[:, : right.shape[1]], prod[:, right.shape[1] :]

    def multiply(number):
        place, first = CHUNKS[number]
        half = first // COLS
        arrived(mates[number], back_recv.at[number])
        weight = w_got[place, 0, 0:1, 0:1]

        def own(h, side):
            parts = [
                blocks[k][pl.ds(16 * side, 16), h].reshape(256, COLS)
                for k in range(n)
                if CHUNKS[k][0] == place
            ]
            return jnp.concatenate(parts, axis=1)

        @pl.loop(0, 2 * ROUNDS)
        def _(i):
            h, r = lax.div(i, ROUNDS), lax.rem(i, ROUNDS)
            src_re, src_im = gram(
                own(h, 0), mates[number][pl.ds(0, 16), r, h].reshape(256, COLS)
            )
            rcv_re, rcv_im = gram(
                own(h, 1), mates[number][pl.ds(16, 16), r, h].reshape(256, COLS)
            )
            term = weight * (src_re * rcv_re - src_im * rcv_im)
            terms[half, pl.ds(h * 8, 8), r] += term.reshape(8, 32, COLS)

    def finish(number):
        arrived(blocks[number].at[pl.ds(0, PEERS - 1)], spread_send.at[number])
        arrived(picked[number].at[pl.ds(0, PEERS - 1)], back_send.at[number])

    def up_copy(half, step, source):
        return pltpu.make_async_remote_copy(
            source, up_in.at[half, step], ring_send.at[0, half, step],
            ring_recv.at[0, half, step], device_id=up, device_id_type=MESH,
        )

    def down_copy(half, step, source):
        return pltpu.make_async_remote_copy(
            source, down_in.at[half, step], ring_send.at[1, half, step],
            ring_recv.at[1, half, step], device_id=down, device_id_type=MESH,
        )

    def ring_start(half):
        up_copy(half, 0, terms.at[half, lax.rem(z + 8, 16)]).start()
        down_copy(half, 0, terms.at[half, lax.rem(z + 9, 16)]).start()

    def ring_step(half, s):
        up_copy(half, s, up_in.at[half, s]).wait_recv()
        up_in[half, s] += terms[half, lax.rem(z + 7 - s, 16)]
        up_copy(half, s + 1, up_in.at[half, s]).start()
        down_copy(half, s, down_in.at[half, s]).wait_recv()
        down_in[half, s] += terms[half, lax.rem(z + 10 + s, 16)]
        if not isinstance(s, int) or s < 6:
            down_copy(half, s + 1, down_in.at[half, s]).start()

    def ring_end(half):
        up_copy(half, 7, up_in.at[half, 7]).wait_recv()
        out_ref[:, :, half * COLS : (half + 1) * COLS] = up_in[half, 7] + down_in[half, 6]

    @pl.when(two)
    def _():
        arrived(w_got.at[1], w_recv.at[1])
        spread(0, ((1, 8, 10),))
        z_steps(1, 18, 6)
        back(0, ((1, 24, 8), (2, 0, 8)))

    @pl.when(jnp.logical_not(two))
    def _():
        z_steps(1, 8, 24)
        z_steps(2, 0, 8)

    arrived(w_got.at[0], w_recv.at[0])
    spread(1, ((2, 8, 8),))
    z_steps(3, 0, 6)
    back(1, ((3, 6, 16),))

    @pl.when(two)
    def _():
        spread(2, ((3, 22, 10),))
        back(2)

    @pl.when(jnp.logical_not(two))
    def _():
        z_steps(3, 22, 10)

    spread(3)

    @pl.when(two)
    def _():
        multiply(0)

    multiply(1)
    ring_start(0)
    back(3)
    ring_step(0, 0)
    ring_step(0, 1)

    @pl.when(two)
    def _():
        multiply(2)

    multiply(3)
    ring_start(1)
    ring_step(0, 2)
    ring_step(1, 0)
    ring_step(0, 3)
    ring_step(1, 1)
    ring_step(0, 4)
    ring_step(1, 2)
    ring_step(0, 5)
    ring_step(1, 3)
    ring_step(0, 6)
    ring_step(1, 4)
    ring_step(1, 5)
    ring_step(1, 6)
    ring_end(0)
    ring_end(1)

    @pl.when(two)
    def _():
        finish(0)
        finish(2)

    finish(1)
    finish(3)
    for number in range(n):
        launched(number)
    arrived(w_own, w_send)

    for half in range(2):
        for step in range(8):
            up_copy(half, step, up_in.at[half, step]).wait_send()
        for step in range(7):
            down_copy(half, step, down_in.at[half, step]).wait_send()


def on_device(green_src, green_rcv, pairing, freq_index):
    bf16, f32 = jnp.bfloat16, jnp.float32
    n = len(CHUNKS)
    dma = pltpu.SemaphoreType.DMA
    result = pl.pallas_call(
        kernel,
        out_shape=jax.ShapeDtypeStruct((ROUNDS, 32, 256), f32),
        in_specs=[
            pl.BlockSpec(memory_space=pl.ANY),
            pl.BlockSpec(memory_space=pl.ANY),
            pl.BlockSpec(memory_space=pltpu.SMEM),
            pl.BlockSpec(memory_space=pltpu.SMEM),
        ],
        out_specs=pl.BlockSpec(memory_space=pltpu.VMEM),
        scratch_shapes=[
            *(pltpu.VMEM((PEERS, 2, SLICE, COLS), bf16) for _ in CHUNKS),
            *(pltpu.VMEM((4, 8, 2, SLICE, COLS), bf16) for _ in CHUNKS),
            *(pltpu.VMEM((PEERS, ROUNDS, 2, SLICE, COLS), bf16) for _ in CHUNKS),
            *(pltpu.VMEM((PEERS, ROUNDS, 2, SLICE, COLS), bf16) for _ in CHUNKS),
            pltpu.VMEM((3, 8, 128), f32),
            pltpu.VMEM((2, 2, 8, 128), f32),
            pltpu.VMEM((2, 16, ROUNDS, 32, COLS), f32),
            pltpu.VMEM((2, 8, ROUNDS, 32, COLS), f32),
            pltpu.VMEM((2, 7, ROUNDS, 32, COLS), f32),
            dma((n, 2)), dma((n,)), dma, dma((2,)),
            dma((n,)), dma((n,)), dma((n,)), dma((n,)),
            dma((2, 2, 8)), dma((2, 2, 8)),
        ],
        compiler_params=pltpu.CompilerParams(
            collective_id=0, has_side_effects=True, vmem_limit_bytes=60 << 20
        ),
    )(
        green_src.reshape(3, 16, 16, 256), green_rcv.reshape(3, 16, 16, 256),
        pairing, freq_index,
    )
    return result.swapaxes(0, 1)


def solution(mesh):
    in_specs = (P("freq", None, None, "pts"), P("freq", None, None, "pts"), P(), P("freq"))
    out_specs = P(("pts", "freq"), None, None)
    return jax.shard_map(
        on_device, mesh=mesh, in_specs=in_specs, out_specs=out_specs, check_vma=False
    )
```

```python
import functools

import jax
import jax.numpy as jnp
from jax import lax
from jax.experimental import pallas as pl
from jax.experimental.pallas import tpu as pltpu
from jax.sharding import PartitionSpec as P

ROUNDS = 2
FBINS = 64
PEERS = 32
SLICE = 16
MESH = pl.DeviceIdType.MESH
PLACES = (1, 0, 0, 1)
SPREAD = 3
COLS = 128
GATHER = (
    (8, 2), (7, 1), (5, -1), (-5, 1), (-7, -1),
    (4, 2), (3, 1), (-3, -1), (-4, -2), (1, 1), (-1, -1),
)
LEADERS = (6, -6, 2, -2)
NEIGHBOURS = (-6, -4, -2, -1, 1, 2, 4, 6)


def device(x, y_core, z):
    return (x * 16 + lax.div(z, 8) * 8 + y_core, lax.rem(z, 8))


def kernel(src_ref, rcv_ref, pair_ref, freq_ref, out_ref, *scratch):
    n = len(PLACES)
    blocks = scratch[:n]
    slices, picked, mates = (scratch[n + i * SPREAD : n + (i + 1) * SPREAD] for i in range(3))
    (
        w_own, w_got, terms, near, led, last,
        z_send, z_recv, w_send, w_recv, spread_send, spread_recv, back_send, back_recv,
        near_send, near_recv, last_send, last_recv,
    ) = scratch[n + 3 * SPREAD :]
    p, f = lax.axis_index("pts"), lax.axis_index("freq")
    x, zh, yc = lax.div(p, 16), lax.rem(lax.div(p, 8), 2), lax.rem(p, 8)
    z = zh * 8 + f
    me = x * 8 + yc

    def peer(t):
        return (lax.div(t, 8) * 16 + zh * 8 + lax.rem(t, 8), f)

    def plane(shift):
        return lax.rem(z + (shift + 16), 16)

    barrier = pltpu.get_barrier_semaphore()
    for shift in NEIGHBOURS:
        pl.semaphore_signal(
            barrier, inc=1, device_id=device(x, yc, plane(shift)), device_id_type=MESH
        )

    @pl.loop(1, PEERS)
    def _(i):
        pl.semaphore_signal(
            barrier, inc=1, device_id=peer(lax.rem(me + i, PEERS)), device_id_type=MESH
        )

    for slot in range(3):
        scaled = (freq_ref[slot].astype(jnp.float32) + 1.0) / FBINS
        scaled = scaled * scaled
        w_own[slot] = jnp.full(w_own.shape[1:], scaled * scaled, jnp.float32)
    pl.semaphore_wait(barrier, PEERS - 1 + len(NEIGHBOURS))

    far = lax.rem(f + 4, 8)

    def meeting(way):
        return (x * 16 + lax.rem(lax.div(f, 4) + way, 2) * 8 + yc, far)

    def arrived(ref, sem):
        pltpu.make_async_copy(ref, ref, sem).wait()

    def z_step(number, k):
        way, row = lax.rem(k, 2), lax.div(k, 2)
        if PLACES[number]:
            slot, half = 2, way if number == 0 else 1 - way
        else:
            slot, half = way, number - 1
        for side, ref in enumerate((src_ref, rcv_ref)):
            pltpu.make_async_remote_copy(
                ref.at[slot, row, :, pl.ds(pl.multiple_of(half * COLS, COLS), COLS)],
                blocks[number].at[16 * side + row, zh],
                z_send.at[number, side], z_recv.at[number],
                device_id=meeting(way), device_id_type=MESH,
            ).start()

    def z_steps(number, start, count):
        @pl.loop(start, start + count)
        def _(k):
            z_step(number, k)

    def z_between(i, plan):
        for number, start, count in plan:
            before = lax.div((i - 1) * count, PEERS - 1)

            @pl.when(lax.div(i * count, PEERS - 1) > before)
            def _(number=number, k=start + before):
                z_step(number, k)

    def launched(number):
        for side, ref in enumerate((src_ref, rcv_ref)):
            if PLACES[number]:
                arrived(ref.at[pl.ds(2, 1)], z_send.at[number, side])
            else:
                arrived(
                    ref.at[pl.ds(0, 2), :, :, pl.ds((number - 1) * COLS, COLS)],
                    z_send.at[number, side],
                )

    for way in range(2):
        for slot, place in ((2, 1), (way, 0)):
            pltpu.make_async_remote_copy(
                w_own.at[slot], w_got.at[place, zh], w_send.at[place], w_recv.at[place],
                device_id=meeting(way), device_id_type=MESH,
            ).start()
    z_steps(0, 0, 32)
    z_steps(1, 0, 20)
    terms[...] = jnp.zeros_like(terms)
    mine = lax.rem(zh + lax.div(far, 4), 2)

    def spread(number, plan=()):
        arrived(blocks[number], z_recv.at[number])

        @pl.loop(1, PEERS)
        def _(i):
            z_between(i, plan)
            t = lax.rem(me + i * 13, PEERS)
            pltpu.make_async_remote_copy(
                blocks[number].at[t], slices[number].at[x, yc],
                spread_send.at[number], spread_recv.at[number],
                device_id=peer(t), device_id_type=MESH,
            ).start()

        pltpu.make_async_copy(
            blocks[number].at[me], slices[number].at[x, yc], spread_recv.at[number]
        ).start()

    def back(number, plan=()):
        arrived(slices[number], spread_recv.at[number])

        def pick(t):
            for r in range(ROUNDS):
                for h in range(2):
                    m = pair_ref[r, lax.div(t, 8) * 16 + h * 8 + lax.rem(t, 8)]
                    picked[number][t, r, h] = slices[number][
                        lax.div(m, 16), lax.rem(m, 8), lax.rem(lax.div(m, 8), 2)
                    ]

        @pl.loop(1, PEERS)
        def _(i):
            z_between(i, plan)
            t = lax.rem(me + i * 13, PEERS)
            pick(t)
            pltpu.make_async_remote_copy(
                picked[number].at[t], mates[number].at[me],
                back_send.at[number], back_recv.at[number],
                device_id=peer(t), device_id_type=MESH,
            ).start()

        pick(me)
        pltpu.make_async_copy(
            picked[number].at[me], mates[number].at[me], back_recv.at[number]
        ).start()

    def gram(left, right):
        turned = jnp.concatenate([right[128:], -right[:128]], axis=0)
        both = jnp.concatenate([right, turned], axis=1)
        prod = lax.dot_general(
            left, both, (((0,), (0,)), ((), ())), preferred_element_type=jnp.float32
        )
        return prod[:, : right.shape[1]], prod[:, right.shape[1] :]

    def multiply(number):
        arrived(mates[number], back_recv.at[number])
        place = PLACES[number]
        weight = w_got[place, 0, 0:1, 0:1]
        pair = (0, 3) if place else (1, 2)
        first = mine if place else 0
        half = mine if place else number - 1

        def own(h, side):
            parts = [blocks[k][pl.ds(16 * side, 16), h].reshape(256, COLS) for k in pair]
            return jnp.concatenate(parts, axis=1)

        @pl.loop(0, 2 * ROUNDS)
        def _(i):
            h, r = lax.div(i, ROUNDS), lax.rem(i, ROUNDS)
            src_re, src_im = gram(
                own(h, 0), mates[number][pl.ds(0, 16), r, h].reshape(256, COLS)
            )
            rcv_re, rcv_im = gram(
                own(h, 1), mates[number][pl.ds(16, 16), r, h].reshape(256, COLS)
            )
            term = weight * (src_re * rcv_re - src_im * rcv_im)
            term = term.reshape(2, 4, 32, COLS)
            terms[half, pl.ds(h * 8 + 4 * first, 4), r] += term[0]
            terms[half, pl.ds(h * 8 + 4 * (1 - first), 4), r] += term[1]

    def finish(number):
        arrived(blocks[number].at[pl.ds(0, PEERS - 1)], spread_send.at[number])
        arrived(picked[number].at[pl.ds(0, PEERS - 1)], back_send.at[number])

    def gather_copy(half, i):
        dist, shift = GATHER[i]
        return pltpu.make_async_remote_copy(
            terms.at[half, plane(dist)], near.at[half, i],
            near_send.at[half, i], near_recv.at[half, i],
            device_id=device(x, yc, plane(shift)), device_id_type=MESH,
        )

    def lead_copy(half, i):
        return pltpu.make_async_remote_copy(
            led.at[half, i], last.at[half, i], last_send.at[half, i], last_recv.at[half, i],
            device_id=device(x, yc, plane(LEADERS[i])), device_id_type=MESH,
        )

    def gather(half):
        for i in range(len(GATHER)):
            gather_copy(half, i).start()

    def gathered(half, lead):
        total = terms[half, plane(lead)]
        for i, (dist, shift) in enumerate(GATHER):
            if dist - shift == lead:
                gather_copy(half, i).wait_recv()
                total = total + near[half, i]
        return total

    def lead(half):
        for i, dist in enumerate(LEADERS):
            led[half, i] = gathered(half, dist)
            lead_copy(half, i).start()

    def total(half):
        result = gathered(half, 0)
        for i in range(len(LEADERS)):
            lead_copy(half, i).wait_recv()
            result = result + last[half, i]
        out_ref[:, :, half * COLS : (half + 1) * COLS] = result

    for place in range(2):
        arrived(w_got.at[place], w_recv.at[place])
    spread(0, ((1, 20, 12), (2, 0, 2),))
    z_steps(2, 2, 8)
    back(0, ((2, 10, 22),))
    spread(1, ((3, 0, 12),))
    z_steps(3, 12, 6)
    back(1, ((3, 18, 14),))
    spread(2)
    multiply(1)
    back(2)
    arrived(blocks[3], z_recv.at[3])
    multiply(0)
    gather(0)
    lead(0)
    multiply(2)
    gather(1)
    lead(1)
    total(0)
    total(1)

    for number in range(SPREAD):
        finish(number)
    for number in range(n):
        launched(number)
    for place in range(2):
        arrived(w_own.at[pl.ds(0, 2)], w_send.at[place])

    for half in range(2):
        for i in range(len(GATHER)):
            gather_copy(half, i).wait_send()
        for i in range(len(LEADERS)):
            lead_copy(half, i).wait_send()


def on_device(green_src, green_rcv, pairing, freq_index):
    bf16, f32 = jnp.bfloat16, jnp.float32
    n = len(PLACES)
    dma = pltpu.SemaphoreType.DMA
    result = pl.pallas_call(
        kernel,
        out_shape=jax.ShapeDtypeStruct((ROUNDS, 32, 256), f32),
        in_specs=[
            pl.BlockSpec(memory_space=pl.ANY),
            pl.BlockSpec(memory_space=pl.ANY),
            pl.BlockSpec(memory_space=pltpu.SMEM),
            pl.BlockSpec(memory_space=pltpu.SMEM),
        ],
        out_specs=pl.BlockSpec(memory_space=pltpu.VMEM),
        scratch_shapes=[
            *(pltpu.VMEM((PEERS, 2, SLICE, COLS), bf16) for _ in PLACES),
            *(pltpu.VMEM((4, 8, 2, SLICE, COLS), bf16) for _ in range(SPREAD)),
            *(pltpu.VMEM((PEERS, ROUNDS, 2, SLICE, COLS), bf16) for _ in range(SPREAD)),
            *(pltpu.VMEM((PEERS, ROUNDS, 2, SLICE, COLS), bf16) for _ in range(SPREAD)),
            pltpu.VMEM((3, 8, 128), f32),
            pltpu.VMEM((2, 2, 8, 128), f32),
            pltpu.VMEM((2, 16, ROUNDS, 32, COLS), f32),
            pltpu.VMEM((2, len(GATHER), ROUNDS, 32, COLS), f32),
            pltpu.VMEM((2, len(LEADERS), ROUNDS, 32, COLS), f32),
            pltpu.VMEM((2, len(LEADERS), ROUNDS, 32, COLS), f32),
            dma((n, 2)), dma((n,)), dma((2,)), dma((2,)),
            dma((n,)), dma((n,)), dma((n,)), dma((n,)),
            dma((2, len(GATHER))), dma((2, len(GATHER))),
            dma((2, len(LEADERS))), dma((2, len(LEADERS))),
        ],
        compiler_params=pltpu.CompilerParams(
            collective_id=0, has_side_effects=True, vmem_limit_bytes=60 << 20
        ),
    )(
        green_src.reshape(3, 16, 16, 256), green_rcv.reshape(3, 16, 16, 256),
        pairing, freq_index,
    )
    return result.swapaxes(0, 1)


def solution(mesh):
    in_specs = (P("freq", None, None, "pts"), P("freq", None, None, "pts"), P(), P("freq"))
    out_specs = P(("pts", "freq"), None, None)
    return jax.shard_map(
        on_device, mesh=mesh, in_specs=in_specs, out_specs=out_specs, check_vma=False
    )
```

```python
import functools

import jax
import jax.numpy as jnp
from jax import lax
from jax.experimental import pallas as pl
from jax.experimental.pallas import tpu as pltpu
from jax.sharding import PartitionSpec as P

ROUNDS = 2
FBINS = 64
PEERS = 32
SLICE = 16
MESH = pl.DeviceIdType.MESH
PLACES = (1, 0, 0, 1)
GROUP = 2
SPREAD = 3
COLS = 128
GATHER = (
    (8, 2), (7, 1), (5, -1), (-5, 1), (-7, -1),
    (4, 2), (3, 1), (-3, -1), (-4, -2), (1, 1), (-1, -1),
)
LEADERS = (6, -6, 2, -2)
NEIGHBOURS = (-6, -4, -2, -1, 1, 2, 4, 6)


def device(x, y_core, z):
    return (x * 16 + lax.div(z, 8) * 8 + y_core, lax.rem(z, 8))


def kernel(src_ref, rcv_ref, pair_ref, freq_ref, out_ref, *scratch):
    n = len(PLACES)
    blocks = scratch[:n]
    slices, picked, mates = (scratch[n + i * SPREAD : n + (i + 1) * SPREAD] for i in range(3))
    (
        w_own, w_got, terms, near, led, last,
        z_send, z_recv, w_send, w_recv, spread_send, spread_recv, back_send, back_recv,
        near_send, near_recv, last_send, last_recv,
    ) = scratch[n + 3 * SPREAD :]
    p, f = lax.axis_index("pts"), lax.axis_index("freq")
    x, zh, yc = lax.div(p, 16), lax.rem(lax.div(p, 8), 2), lax.rem(p, 8)
    z = zh * 8 + f
    me = x * 8 + yc

    def peer(t):
        return (lax.div(t, 8) * 16 + zh * 8 + lax.rem(t, 8), f)

    def plane(shift):
        return lax.rem(z + (shift + 16), 16)

    barrier = pltpu.get_barrier_semaphore()
    for shift in NEIGHBOURS:
        pl.semaphore_signal(
            barrier, inc=1, device_id=device(x, yc, plane(shift)), device_id_type=MESH
        )

    @pl.loop(1, PEERS)
    def _(i):
        pl.semaphore_signal(
            barrier, inc=1, device_id=peer(lax.rem(me + i, PEERS)), device_id_type=MESH
        )

    for slot in range(3):
        scaled = (freq_ref[slot].astype(jnp.float32) + 1.0) / FBINS
        scaled = scaled * scaled
        w_own[slot] = jnp.full(w_own.shape[1:], scaled * scaled, jnp.float32)
    pl.semaphore_wait(barrier, PEERS - 1 + len(NEIGHBOURS))

    far = lax.rem(f + 4, 8)

    def meeting(way):
        return (x * 16 + lax.rem(lax.div(f, 4) + way, 2) * 8 + yc, far)

    def arrived(ref, sem):
        pltpu.make_async_copy(ref, ref, sem).wait()

    def z_step(number, k):
        way, row = lax.rem(k, 2), lax.div(k, 2) * GROUP
        rows = pl.ds(row, GROUP)
        if PLACES[number]:
            slot, half = 2, way if number == 0 else 1 - way
        else:
            slot, half = way, number - 1
        for side, ref in enumerate((src_ref, rcv_ref)):
            pltpu.make_async_remote_copy(
                ref.at[slot, rows, :, pl.ds(pl.multiple_of(half * COLS, COLS), COLS)],
                blocks[number].at[pl.ds(16 * side + row, GROUP), zh],
                z_send.at[number, side], z_recv.at[number],
                device_id=meeting(way), device_id_type=MESH,
            ).start()

    def z_steps(number, start, count):
        @pl.loop(start, start + count)
        def _(k):
            z_step(number, k)

    def z_between(i, plan):
        for number, start, count in plan:
            before = lax.div((i - 1) * count, PEERS - 1)

            @pl.when(lax.div(i * count, PEERS - 1) > before)
            def _(number=number, k=start + before):
                z_step(number, k)

    def launched(number):
        for side, ref in enumerate((src_ref, rcv_ref)):
            if PLACES[number]:
                arrived(ref.at[pl.ds(2, 1)], z_send.at[number, side])
            else:
                arrived(
                    ref.at[pl.ds(0, 2), :, :, pl.ds((number - 1) * COLS, COLS)],
                    z_send.at[number, side],
                )

    for way in range(2):
        for slot, place in ((2, 1), (way, 0)):
            pltpu.make_async_remote_copy(
                w_own.at[slot], w_got.at[place, zh], w_send.at[place], w_recv.at[place],
                device_id=meeting(way), device_id_type=MESH,
            ).start()
    z_steps(0, 0, 16)
    z_steps(1, 0, 10)
    terms[...] = jnp.zeros_like(terms)
    mine = lax.rem(zh + lax.div(far, 4), 2)

    def spread(number, plan=()):
        arrived(blocks[number], z_recv.at[number])

        @pl.loop(1, PEERS)
        def _(i):
            z_between(i, plan)
            t = lax.rem(me + i * 13, PEERS)
            pltpu.make_async_remote_copy(
                blocks[number].at[t], slices[number].at[x, yc],
                spread_send.at[number], spread_recv.at[number],
                device_id=peer(t), device_id_type=MESH,
            ).start()

        pltpu.make_async_copy(
            blocks[number].at[me], slices[number].at[x, yc], spread_recv.at[number]
        ).start()

    def back(number, plan=()):
        arrived(slices[number], spread_recv.at[number])

        def pick(t):
            for r in range(ROUNDS):
                for h in range(2):
                    m = pair_ref[r, lax.div(t, 8) * 16 + h * 8 + lax.rem(t, 8)]
                    picked[number][t, r, h] = slices[number][
                        lax.div(m, 16), lax.rem(m, 8), lax.rem(lax.div(m, 8), 2)
                    ]

        @pl.loop(1, PEERS)
        def _(i):
            z_between(i, plan)
            t = lax.rem(me + i * 13, PEERS)
            pick(t)
            pltpu.make_async_remote_copy(
                picked[number].at[t], mates[number].at[me],
                back_send.at[number], back_recv.at[number],
                device_id=peer(t), device_id_type=MESH,
            ).start()

        pick(me)
        pltpu.make_async_copy(
            picked[number].at[me], mates[number].at[me], back_recv.at[number]
        ).start()

    def gram(left, right):
        turned = jnp.concatenate([right[128:], -right[:128]], axis=0)
        both = jnp.concatenate([right, turned], axis=1)
        prod = lax.dot_general(
            left, both, (((0,), (0,)), ((), ())), preferred_element_type=jnp.float32
        )
        return prod[:, : right.shape[1]], prod[:, right.shape[1] :]

    def multiply(number):
        arrived(mates[number], back_recv.at[number])
        place = PLACES[number]
        weight = w_got[place, 0, 0:1, 0:1]
        pair = (0, 3) if place else (1, 2)
        first = mine if place else 0
        half = mine if place else number - 1

        def own(h, side):
            parts = [blocks[k][pl.ds(16 * side, 16), h].reshape(256, COLS) for k in pair]
            return jnp.concatenate(parts, axis=1)

        @pl.loop(0, 2 * ROUNDS)
        def _(i):
            h, r = lax.div(i, ROUNDS), lax.rem(i, ROUNDS)
            src_re, src_im = gram(
                own(h, 0), mates[number][pl.ds(0, 16), r, h].reshape(256, COLS)
            )
            rcv_re, rcv_im = gram(
                own(h, 1), mates[number][pl.ds(16, 16), r, h].reshape(256, COLS)
            )
            term = weight * (src_re * rcv_re - src_im * rcv_im)
            term = term.reshape(2, 4, 32, COLS)
            terms[half, pl.ds(h * 8 + 4 * first, 4), r] += term[0]
            terms[half, pl.ds(h * 8 + 4 * (1 - first), 4), r] += term[1]

    def finish(number):
        arrived(blocks[number].at[pl.ds(0, PEERS - 1)], spread_send.at[number])
        arrived(picked[number].at[pl.ds(0, PEERS - 1)], back_send.at[number])

    def gather_copy(half, i):
        dist, shift = GATHER[i]
        return pltpu.make_async_remote_copy(
            terms.at[half, plane(dist)], near.at[half, i],
            near_send.at[half, i], near_recv.at[half, i],
            device_id=device(x, yc, plane(shift)), device_id_type=MESH,
        )

    def lead_copy(half, i):
        return pltpu.make_async_remote_copy(
            led.at[half, i], last.at[half, i], last_send.at[half, i], last_recv.at[half, i],
            device_id=device(x, yc, plane(LEADERS[i])), device_id_type=MESH,
        )

    def gather(half):
        for i in range(len(GATHER)):
            gather_copy(half, i).start()

    def gathered(half, lead):
        total = terms[half, plane(lead)]
        for i, (dist, shift) in enumerate(GATHER):
            if dist - shift == lead:
                gather_copy(half, i).wait_recv()
                total = total + near[half, i]
        return total

    def lead(half):
        for i, dist in enumerate(LEADERS):
            led[half, i] = gathered(half, dist)
            lead_copy(half, i).start()

    def total(half):
        result = gathered(half, 0)
        for i in range(len(LEADERS)):
            lead_copy(half, i).wait_recv()
            result = result + last[half, i]
        out_ref[:, :, half * COLS : (half + 1) * COLS] = result

    for place in range(2):
        arrived(w_got.at[place], w_recv.at[place])
    spread(0, ((1, 10, 6), (2, 0, 1),))
    z_steps(2, 1, 4)
    back(0, ((2, 5, 11),))
    spread(1, ((3, 0, 6),))
    z_steps(3, 6, 3)
    back(1, ((3, 9, 7),))
    spread(2)
    multiply(1)
    arrived(blocks[3], z_recv.at[3])
    multiply(0)
    gather(0)
    back(2)
    lead(0)
    multiply(2)
    gather(1)
    lead(1)
    total(0)
    total(1)

    for number in range(SPREAD):
        finish(number)
    for number in range(n):
        launched(number)
    for place in range(2):
        arrived(w_own.at[pl.ds(0, 2)], w_send.at[place])

    for half in range(2):
        for i in range(len(GATHER)):
            gather_copy(half, i).wait_send()
        for i in range(len(LEADERS)):
            lead_copy(half, i).wait_send()


def on_device(green_src, green_rcv, pairing, freq_index):
    bf16, f32 = jnp.bfloat16, jnp.float32
    n = len(PLACES)
    dma = pltpu.SemaphoreType.DMA
    result = pl.pallas_call(
        kernel,
        out_shape=jax.ShapeDtypeStruct((ROUNDS, 32, 256), f32),
        in_specs=[
            pl.BlockSpec(memory_space=pl.ANY),
            pl.BlockSpec(memory_space=pl.ANY),
            pl.BlockSpec(memory_space=pltpu.SMEM),
            pl.BlockSpec(memory_space=pltpu.SMEM),
        ],
        out_specs=pl.BlockSpec(memory_space=pltpu.VMEM),
        scratch_shapes=[
            *(pltpu.VMEM((PEERS, 2, SLICE, COLS), bf16) for _ in PLACES),
            *(pltpu.VMEM((4, 8, 2, SLICE, COLS), bf16) for _ in range(SPREAD)),
            *(pltpu.VMEM((PEERS, ROUNDS, 2, SLICE, COLS), bf16) for _ in range(SPREAD)),
            *(pltpu.VMEM((PEERS, ROUNDS, 2, SLICE, COLS), bf16) for _ in range(SPREAD)),
            pltpu.VMEM((3, 8, 128), f32),
            pltpu.VMEM((2, 2, 8, 128), f32),
            pltpu.VMEM((2, 16, ROUNDS, 32, COLS), f32),
            pltpu.VMEM((2, len(GATHER), ROUNDS, 32, COLS), f32),
            pltpu.VMEM((2, len(LEADERS), ROUNDS, 32, COLS), f32),
            pltpu.VMEM((2, len(LEADERS), ROUNDS, 32, COLS), f32),
            dma((n, 2)), dma((n,)), dma((2,)), dma((2,)),
            dma((n,)), dma((n,)), dma((n,)), dma((n,)),
            dma((2, len(GATHER))), dma((2, len(GATHER))),
            dma((2, len(LEADERS))), dma((2, len(LEADERS))),
        ],
        compiler_params=pltpu.CompilerParams(
            collective_id=0, has_side_effects=True, vmem_limit_bytes=60 << 20
        ),
    )(
        green_src.reshape(3, 16, 16, 256), green_rcv.reshape(3, 16, 16, 256),
        pairing, freq_index,
    )
    return result.swapaxes(0, 1)


def solution(mesh):
    in_specs = (P("freq", None, None, "pts"), P("freq", None, None, "pts"), P(), P("freq"))
    out_specs = P(("pts", "freq"), None, None)
    return jax.shard_map(
        on_device, mesh=mesh, in_specs=in_specs, out_specs=out_specs, check_vma=False
    )
```

```python
import functools

import jax
import jax.numpy as jnp
from jax import lax
from jax.experimental import pallas as pl
from jax.experimental.pallas import tpu as pltpu
from jax.sharding import PartitionSpec as P

ROUNDS = 2
FBINS = 64
PEERS = 32
SLICE = 16
MESH = pl.DeviceIdType.MESH
PLACES = (1, 0, 0, 1)
GROUP = 2
SPREAD = 3
COLS = 128
GATHER = (
    (8, 2), (7, 1), (5, -1), (-5, 1), (-7, -1),
    (4, 2), (3, 1), (-3, -1), (-4, -2), (1, 1), (-1, -1),
)
LEADERS = (6, -6, 2, -2)
NEIGHBOURS = (-6, -4, -2, -1, 1, 2, 4, 6)


def device(x, y_core, z):
    return (x * 16 + lax.div(z, 8) * 8 + y_core, lax.rem(z, 8))


def kernel(src_ref, rcv_ref, pair_ref, freq_ref, out_ref, *scratch):
    n = len(PLACES)
    blocks = scratch[:n]
    slices, picked, mates = (scratch[n + i * SPREAD : n + (i + 1) * SPREAD] for i in range(3))
    (
        w_own, w_got, terms, near, led, last,
        z_send, z_recv, w_send, w_recv, spread_send, spread_recv, back_send, back_recv,
        near_send, near_recv, last_send, last_recv,
    ) = scratch[n + 3 * SPREAD :]
    p, f = lax.axis_index("pts"), lax.axis_index("freq")
    x, zh, yc = lax.div(p, 16), lax.rem(lax.div(p, 8), 2), lax.rem(p, 8)
    z = zh * 8 + f
    me = x * 8 + yc

    def peer(t):
        return (lax.div(t, 8) * 16 + zh * 8 + lax.rem(t, 8), f)

    def plane(shift):
        return lax.rem(z + (shift + 16), 16)

    barrier = pltpu.get_barrier_semaphore()
    for shift in NEIGHBOURS:
        pl.semaphore_signal(
            barrier, inc=1, device_id=device(x, yc, plane(shift)), device_id_type=MESH
        )

    @pl.loop(1, PEERS)
    def _(i):
        pl.semaphore_signal(
            barrier, inc=1, device_id=peer(lax.rem(me + i, PEERS)), device_id_type=MESH
        )

    for slot in range(3):
        scaled = (freq_ref[slot].astype(jnp.float32) + 1.0) / FBINS
        scaled = scaled * scaled
        w_own[slot] = jnp.full(w_own.shape[1:], scaled * scaled, jnp.float32)
    pl.semaphore_wait(barrier, PEERS - 1 + len(NEIGHBOURS))

    far = lax.rem(f + 4, 8)

    def meeting(way):
        return (x * 16 + lax.rem(lax.div(f, 4) + way, 2) * 8 + yc, far)

    def arrived(ref, sem):
        pltpu.make_async_copy(ref, ref, sem).wait()

    def z_step(number, k):
        way, row = lax.rem(k, 2), lax.div(k, 2) * GROUP
        rows = pl.ds(row, GROUP)
        if PLACES[number]:
            slot, half = 2, way if number == 0 else 1 - way
        else:
            slot, half = way, number - 1
        for side, ref in enumerate((src_ref, rcv_ref)):
            pltpu.make_async_remote_copy(
                ref.at[slot, rows, :, pl.ds(pl.multiple_of(half * COLS, COLS), COLS)],
                blocks[number].at[pl.ds(16 * side + row, GROUP), zh],
                z_send.at[number, side], z_recv.at[number],
                device_id=meeting(way), device_id_type=MESH,
            ).start()

    def z_steps(number, start, count):
        @pl.loop(start, start + count)
        def _(k):
            z_step(number, k)

    def z_between(i, plan):
        for number, start, count in plan:
            before = lax.div((i - 1) * count, PEERS - 1)

            @pl.when(lax.div(i * count, PEERS - 1) > before)
            def _(number=number, k=start + before):
                z_step(number, k)

    def launched(number):
        for side, ref in enumerate((src_ref, rcv_ref)):
            if PLACES[number]:
                arrived(ref.at[pl.ds(2, 1)], z_send.at[number, side])
            else:
                arrived(
                    ref.at[pl.ds(0, 2), :, :, pl.ds((number - 1) * COLS, COLS)],
                    z_send.at[number, side],
                )

    for way in range(2):
        for slot, place in ((2, 1), (way, 0)):
            pltpu.make_async_remote_copy(
                w_own.at[slot], w_got.at[place, zh], w_send.at[place], w_recv.at[place],
                device_id=meeting(way), device_id_type=MESH,
            ).start()
    z_steps(0, 0, 16)
    z_steps(1, 0, 10)
    terms[...] = jnp.zeros_like(terms)
    mine = lax.rem(zh + lax.div(far, 4), 2)

    def spread(number, plan=()):
        arrived(blocks[number], z_recv.at[number])

        @pl.loop(1, PEERS)
        def _(i):
            z_between(i, plan)
            t = lax.rem(me + i * 13, PEERS)
            pltpu.make_async_remote_copy(
                blocks[number].at[t], slices[number].at[x, yc],
                spread_send.at[number], spread_recv.at[number],
                device_id=peer(t), device_id_type=MESH,
            ).start()

        pltpu.make_async_copy(
            blocks[number].at[me], slices[number].at[x, yc], spread_recv.at[number]
        ).start()

    def back(number, plan=()):
        arrived(slices[number], spread_recv.at[number])

        def pick(t):
            for r in range(ROUNDS):
                for h in range(2):
                    m = pair_ref[r, lax.div(t, 8) * 16 + h * 8 + lax.rem(t, 8)]
                    picked[number][t, r, h] = slices[number][
                        lax.div(m, 16), lax.rem(m, 8), lax.rem(lax.div(m, 8), 2)
                    ]

        @pl.loop(1, PEERS)
        def _(i):
            z_between(i, plan)
            t = lax.rem(me + i * 13, PEERS)
            pick(t)
            pltpu.make_async_remote_copy(
                picked[number].at[t], mates[number].at[me],
                back_send.at[number], back_recv.at[number],
                device_id=peer(t), device_id_type=MESH,
            ).start()

        pick(me)
        pltpu.make_async_copy(
            picked[number].at[me], mates[number].at[me], back_recv.at[number]
        ).start()

    def gram(left, right):
        turned = jnp.concatenate([right[128:], -right[:128]], axis=0)
        both = jnp.concatenate([right, turned], axis=1)
        prod = lax.dot_general(
            left, both, (((0,), (0,)), ((), ())), preferred_element_type=jnp.float32
        )
        return prod[:, : right.shape[1]], prod[:, right.shape[1] :]

    def multiply(number):
        arrived(mates[number], back_recv.at[number])
        place = PLACES[number]
        weight = w_got[place, 0, 0:1, 0:1]
        pair = (0, 3) if place else (1, 2)
        first = mine if place else 0
        half = mine if place else number - 1

        def own(h, side):
            parts = [blocks[k][pl.ds(16 * side, 16), h].reshape(256, COLS) for k in pair]
            return jnp.concatenate(parts, axis=1)

        @pl.loop(0, 2 * ROUNDS)
        def _(i):
            h, r = lax.div(i, ROUNDS), lax.rem(i, ROUNDS)
            src_re, src_im = gram(
                own(h, 0), mates[number][pl.ds(0, 16), r, h].reshape(256, COLS)
            )
            rcv_re, rcv_im = gram(
                own(h, 1), mates[number][pl.ds(16, 16), r, h].reshape(256, COLS)
            )
            term = weight * (src_re * rcv_re - src_im * rcv_im)
            term = term.reshape(2, 4, 32, COLS)
            terms[half, pl.ds(h * 8 + 4 * first, 4), r] += term[0]
            terms[half, pl.ds(h * 8 + 4 * (1 - first), 4), r] += term[1]

    def finish(number):
        arrived(blocks[number].at[pl.ds(0, PEERS - 1)], spread_send.at[number])
        arrived(picked[number].at[pl.ds(0, PEERS - 1)], back_send.at[number])

    def gather_copy(half, i):
        dist, shift = GATHER[i]
        return pltpu.make_async_remote_copy(
            terms.at[half, plane(dist)], near.at[half, i],
            near_send.at[half, i], near_recv.at[half, i],
            device_id=device(x, yc, plane(shift)), device_id_type=MESH,
        )

    def lead_copy(half, i):
        return pltpu.make_async_remote_copy(
            led.at[half, i], last.at[half, i], last_send.at[half, i], last_recv.at[half, i],
            device_id=device(x, yc, plane(LEADERS[i])), device_id_type=MESH,
        )

    def gather(half):
        for i in range(len(GATHER)):
            gather_copy(half, i).start()

    def gathered(half, lead):
        total = terms[half, plane(lead)]
        for i, (dist, shift) in enumerate(GATHER):
            if dist - shift == lead:
                gather_copy(half, i).wait_recv()
                total = total + near[half, i]
        return total

    def lead(half):
        for i, dist in enumerate(LEADERS):
            led[half, i] = gathered(half, dist)
            lead_copy(half, i).start()

    def total(half):
        result = gathered(half, 0)
        for i in range(len(LEADERS)):
            lead_copy(half, i).wait_recv()
            result = result + last[half, i]
        out_ref[:, :, half * COLS : (half + 1) * COLS] = result

    for place in range(2):
        arrived(w_got.at[place], w_recv.at[place])
    spread(0, ((1, 10, 6), (2, 0, 1),))
    z_steps(2, 1, 4)
    back(0, ((2, 5, 11),))
    spread(1, ((3, 0, 6),))
    z_steps(3, 6, 3)
    back(1, ((3, 9, 7),))
    spread(2)
    multiply(1)
    arrived(blocks[3], z_recv.at[3])
    multiply(0)
    gather(0)
    back(2)
    multiply(2)
    gather(1)
    lead(0)
    lead(1)
    total(0)
    total(1)

    for number in range(SPREAD):
        finish(number)
    for number in range(n):
        launched(number)
    for place in range(2):
        arrived(w_own.at[pl.ds(0, 2)], w_send.at[place])

    for half in range(2):
        for i in range(len(GATHER)):
            gather_copy(half, i).wait_send()
        for i in range(len(LEADERS)):
            lead_copy(half, i).wait_send()


def on_device(green_src, green_rcv, pairing, freq_index):
    bf16, f32 = jnp.bfloat16, jnp.float32
    n = len(PLACES)
    dma = pltpu.SemaphoreType.DMA
    result = pl.pallas_call(
        kernel,
        out_shape=jax.ShapeDtypeStruct((ROUNDS, 32, 256), f32),
        in_specs=[
            pl.BlockSpec(memory_space=pl.ANY),
            pl.BlockSpec(memory_space=pl.ANY),
            pl.BlockSpec(memory_space=pltpu.SMEM),
            pl.BlockSpec(memory_space=pltpu.SMEM),
        ],
        out_specs=pl.BlockSpec(memory_space=pltpu.VMEM),
        scratch_shapes=[
            *(pltpu.VMEM((PEERS, 2, SLICE, COLS), bf16) for _ in PLACES),
            *(pltpu.VMEM((4, 8, 2, SLICE, COLS), bf16) for _ in range(SPREAD)),
            *(pltpu.VMEM((PEERS, ROUNDS, 2, SLICE, COLS), bf16) for _ in range(SPREAD)),
            *(pltpu.VMEM((PEERS, ROUNDS, 2, SLICE, COLS), bf16) for _ in range(SPREAD)),
            pltpu.VMEM((3, 8, 128), f32),
            pltpu.VMEM((2, 2, 8, 128), f32),
            pltpu.VMEM((2, 16, ROUNDS, 32, COLS), f32),
            pltpu.VMEM((2, len(GATHER), ROUNDS, 32, COLS), f32),
            pltpu.VMEM((2, len(LEADERS), ROUNDS, 32, COLS), f32),
            pltpu.VMEM((2, len(LEADERS), ROUNDS, 32, COLS), f32),
            dma((n, 2)), dma((n,)), dma((2,)), dma((2,)),
            dma((n,)), dma((n,)), dma((n,)), dma((n,)),
            dma((2, len(GATHER))), dma((2, len(GATHER))),
            dma((2, len(LEADERS))), dma((2, len(LEADERS))),
        ],
        compiler_params=pltpu.CompilerParams(
            collective_id=0, has_side_effects=True, vmem_limit_bytes=60 << 20
        ),
    )(
        green_src.reshape(3, 16, 16, 256), green_rcv.reshape(3, 16, 16, 256),
        pairing, freq_index,
    )
    return result.swapaxes(0, 1)


def solution(mesh):
    in_specs = (P("freq", None, None, "pts"), P("freq", None, None, "pts"), P(), P("freq"))
    out_specs = P(("pts", "freq"), None, None)
    return jax.shard_map(
        on_device, mesh=mesh, in_specs=in_specs, out_specs=out_specs, check_vma=False
    )
```
